32 devices in a mesh: col: 8 (over z, x), row: 4 (over y, core).
Axes of the slice: x: 2, y: 2, z: 4, core: 2. Of those that a mesh axis runs over, the one named last changes fastest.
Arguments:
- jacobian: float32 [1024, 1024], P(('col', 'row')), may hold values from -6 to 6
- counts: int32 [1024], P(('col', 'row')), may hold values from 0 to 2
Outputs:
- factored: float32 [8, 4, 32, 1, 8, 128], P(None, 'row', None, None, 'col')
- r_rows: float32 [256, 1, 8, 128], P(None, None, 'col')
The draws below stay inside these ranges and needn't reach their ends.
All inputs are finite; a program needn't handle non-finite values.
Results may differ from the reference program's by a relative error of at most 0.0003.
Values sent between devices are 32-bit elements; how exact they have to be, the bound alone decides.
A program may use at most 64 MiB of HBM per device.

```python
import math
import jax
import jax.numpy as jnp
from jax import lax

ROWS_DEV = 32
BLOCK = 128
BLOCKS_DEV = 1
PANELS = 2
ROWS = 1024
COLS = 1024
N_COL = 8
N_ROW = 4


def with_ends(values, stream_key, least, largest):
    spot = [jax.random.randint(jax.random.fold_in(stream_key, axis), (), 0, length) for axis, length in enumerate(values.shape)]
    main_axis = values.shape.index(max(values.shape))
    next_to = spot[:main_axis] + [(spot[main_axis] + 1) % values.shape[main_axis]] + spot[main_axis + 1:]
    return values.at[tuple(spot)].set(least).at[tuple(next_to)].set(largest)


def steps_of(stream_key, dims, shards, least, high):
    level, own = 1.0, jax.random.fold_in(stream_key, 6)
    for axis_at, parts in shards:
        steps = jnp.exp(jax.random.uniform(jax.random.fold_in(own, axis_at), (parts,), jnp.float32, least / len(shards), high / len(shards)))
        level = level * jnp.repeat(steps, dims[axis_at] // parts).reshape([-1 if axis == axis_at else 1 for axis in range(len(dims))])
    return level


def bell_draw(own_key, shape, spread, reach, split=(), held_as=jnp.bfloat16):
    entries = jax.random.normal(own_key, shape, jnp.float32) * spread
    if len(split) > 0:
        entries = steps_of(own_key, shape, split, -0.22, 0.18) * entries
    return jnp.clip(entries, min=-reach, max=reach).astype(held_as)


def setup_inputs(seed: int = 0) -> dict:
    splits = jax.random.split(jax.random.key(seed), 3)
    jacobian = bell_draw(splits[0], (ROWS, COLS), 1.0, 6.0, ((0, 32),), jnp.float32)
    counts = with_ends(jax.random.randint(splits[1], (ROWS,), 0, 3), jax.random.fold_in(splits[1], 1), 0, 2).astype(jnp.int32)
    return dict(jacobian=jacobian, counts=counts)


def reference(jacobian, counts):
    scaled = jacobian * jnp.sqrt(counts.astype(jnp.float32))[:, None]
    matrix = scaled
    column_ids = jnp.arange(COLS)
    stretch = math.sqrt(ROWS)
    couplings = []
    for panel_step in range(PANELS):
        begin_col = panel_step * BLOCK
        end_col = begin_col + BLOCK
        basis, triangle = jnp.linalg.qr(matrix[:, begin_col:end_col])
        sign_fix = jnp.sign(jnp.diagonal(triangle))
        basis = basis * sign_fix[None, :]
        triangle = triangle * sign_fix[:, None]
        coupling = jnp.dot(basis.T.astype(jnp.float32), matrix.astype(jnp.float32), precision=lax.Precision.HIGHEST, preferred_element_type=jnp.float32)
        coupling = jnp.where(column_ids[None, :] < begin_col, jnp.zeros_like(coupling), coupling)
        coupling = coupling.at[:, begin_col:end_col].set(triangle)
        update = matrix - jnp.dot(basis.astype(jnp.float32), coupling.astype(jnp.float32), precision=lax.Precision.HIGHEST, preferred_element_type=jnp.float32)
        matrix = jnp.where(column_ids[None, :] >= end_col, update, matrix)
        matrix = matrix.at[:, begin_col:end_col].set(basis * stretch)
        couplings.append(coupling)
    factored = matrix.reshape(N_COL, N_ROW, ROWS_DEV, BLOCKS_DEV, N_COL, BLOCK)
    r_rows = jnp.concatenate(couplings, 0).reshape(PANELS * BLOCK, BLOCKS_DEV, N_COL, BLOCK)
    return (factored, r_rows)
```

```python
import functools
import math

import jax
import jax.numpy as jnp
from jax import lax
from jax.experimental import pallas as pl
from jax.experimental.pallas import tpu as pltpu
from jax.sharding import PartitionSpec as P

BLOCK = 128
WIDE = 2 * BLOCK
HALF = BLOCK // 2
HIGH = lax.Precision.HIGHEST
MESH = pl.DeviceIdType.MESH
F32 = jnp.float32


def mm(a, b, ca=1, cb=0):
    return lax.dot_general(
        a, b, (((ca,), (cb,)), ((), ())), precision=HIGH, preferred_element_type=F32
    )


def exchange_kernel(
    n_col, chunk, jac, cnt, pan, own, gt, gb,
    sc, part_t, part_b, half_t, half_b, in_t, in_b, out_t, out_b,
    send_p, recv_p, send_a, recv_a, send_r, recv_r,
):
    rows = jac.shape[0]
    c = lax.axis_index("col")
    r = lax.axis_index("row")
    core = lax.rem(r, 2)
    sib = r + 1 - 2 * core
    across = lax.rem(r + 2, 4)

    barrier = pltpu.get_barrier_semaphore()

    def greet(i, carry):
        pl.semaphore_signal(
            barrier, inc=1, device_id=(lax.rem(c + i, n_col), r), device_id_type=MESH
        )
        return carry

    lax.fori_loop(1, n_col, greet, 0)
    for other in (sib, across):
        pl.semaphore_signal(barrier, inc=1, device_id=(c, other), device_id_type=MESH)

    root = jnp.sqrt(cnt[...].astype(F32))
    spread = jnp.broadcast_to(root, (rows, rows))
    eye = lax.broadcasted_iota(jnp.int32, (rows, rows), 0) == lax.broadcasted_iota(
        jnp.int32, (rows, rows), 1
    )
    column = jnp.sum(jnp.where(eye, spread, 0.0), axis=1, keepdims=True)
    sc[...] = jac[...] * column
    mine = pl.ds(pl.multiple_of(c * rows, rows), rows)

    pl.semaphore_wait(barrier, n_col + 1)

    def send_panel(i):
        return pltpu.make_async_remote_copy(
            src_ref=sc.at[:, pl.ds(0, WIDE)],
            dst_ref=pan.at[mine, :],
            send_sem=send_p.at[i],
            recv_sem=recv_p.at[i],
            device_id=(lax.rem(c + i, n_col), r),
            device_id_type=MESH,
        )

    def send_own(i):
        t = lax.rem(c + i, n_col)
        return pltpu.make_async_remote_copy(
            src_ref=sc.at[:, pl.ds(pl.multiple_of(t * BLOCK, BLOCK), BLOCK)],
            dst_ref=own.at[mine, :],
            send_sem=send_a.at[i],
            recv_sem=recv_a.at[i],
            device_id=(t, r),
            device_id_type=MESH,
        )

    def loop(body):
        def step(i, carry):
            body(i)
            return carry

        lax.fori_loop(1, n_col, step, 0)

    loop(lambda i: send_panel(i).start())
    loop(lambda i: send_own(i).start())
    pan[mine, :] = sc[:, :WIDE]
    own[mine, :] = sc[:, pl.ds(pl.multiple_of(c * BLOCK, BLOCK), BLOCK)]
    loop(lambda i: send_panel(i).wait_recv())
    part_t[...] = jnp.zeros_like(part_t)
    part_b[...] = jnp.zeros_like(part_b)

    def gram_panel(k, carry):
        at = pl.ds(pl.multiple_of(k * chunk, chunk), chunk)
        p0, p1 = pan[at, :BLOCK], pan[at, BLOCK:]
        part_t[:, :BLOCK] += mm(p0, p0, 0, 0)
        part_t[:, BLOCK:WIDE] += mm(p0, p1, 0, 0)
        part_b[:, :BLOCK] += mm(p1, p1, 0, 0)
        return carry

    lax.fori_loop(0, n_col * rows // chunk, gram_panel, 0)
    loop(lambda i: send_own(i).wait_recv())

    def gram_own(k, carry):
        at = pl.ds(pl.multiple_of(k * chunk, chunk), chunk)
        a = own[at, :]
        part_t[:, WIDE:] += mm(pan[at, :BLOCK], a, 0, 0)
        part_b[:, BLOCK:] += mm(pan[at, BLOCK:], a, 0, 0)
        return carry

    lax.fori_loop(0, n_col * rows // chunk, gram_own, 0)

    here = pl.ds(pl.multiple_of(core * HALF, HALF), HALF)
    there = pl.ds(pl.multiple_of((1 - core) * HALF, HALF), HALF)

    def swap(src, dst, slot, other):
        return pltpu.make_async_remote_copy(
            src_ref=src,
            dst_ref=dst,
            send_sem=send_r.at[slot],
            recv_sem=recv_r.at[slot],
            device_id=(c, other),
            device_id_type=MESH,
        )

    first = [
        swap(part_t.at[there, :], in_t, 0, sib),
        swap(part_b.at[there, :], in_b, 1, sib),
    ]
    for copy in first:
        copy.start()
    first[0].wait_recv()
    half_t[...] = part_t[here, :] + in_t[...]
    second = [swap(half_t, out_t, 2, across), swap(half_b, out_b, 3, across)]
    second[0].start()
    first[1].wait_recv()
    half_b[...] = part_b[here, :] + in_b[...]
    second[1].start()
    second[0].wait_recv()
    gt[here, :] = half_t[...] + out_t[...]
    third = [
        swap(gt.at[here, :], gt.at[here, :], 4, sib),
        swap(gb.at[here, :], gb.at[here, :], 5, sib),
    ]
    third[0].start()
    second[1].wait_recv()
    gb[here, :] = half_b[...] + out_b[...]
    third[1].start()
    for copy in third:
        copy.wait_recv()
    for copy in first + second + third:
        copy.wait_send()
    loop(lambda i: send_panel(i).wait_send())
    loop(lambda i: send_own(i).wait_send())


def eliminate(m):
    row = lax.broadcasted_iota(jnp.int32, (8, BLOCK), 0)
    for kb in range(BLOCK // 8):
        r0 = 8 * kb
        left = m[r0 : r0 + 8, :BLOCK]
        right = m[r0 : r0 + 8, BLOCK:]
        cols = [jnp.broadcast_to(left[:, r0 + k : r0 + k + 1], (8, BLOCK)) for k in range(8)]
        diag = jnp.zeros((8, BLOCK), F32)
        for k in range(8):
            pivot = jnp.broadcast_to(cols[k][k : k + 1, :], (8, BLOCK))
            diag = jnp.where(row == k, pivot, diag)
            if k < 7:
                factor = jnp.where(row > k, cols[k] / pivot, 0.0)
                for j in range(k + 1, 8):
                    cols[j] = cols[j] - factor * cols[j][k : k + 1, :]
                left = left - factor * left[k : k + 1, :]
                right = right - factor * right[k : k + 1, :]
        scale = lax.rsqrt(diag)
        left = left * scale
        right = right * scale
        m[r0 : r0 + 8, :BLOCK] = left
        m[r0 : r0 + 8, BLOCK:] = right
        if kb < BLOCK // 8 - 1:
            after = mm(left, jnp.concatenate([left, right], axis=1), 0, 0)
            m[r0 + 8 :, :] -= after[r0 + 8 :, :]


def finish_kernel(n_col, stretch, chunk, pan, own, gt, gb, fac, rr, m):
    c = lax.axis_index("col")
    at_row = lax.broadcasted_iota(jnp.int32, (BLOCK, BLOCK), 0)
    at_col = lax.broadcasted_iota(jnp.int32, (BLOCK, BLOCK), 1)
    eye = jnp.where(at_row == at_col, 1.0, 0.0).astype(F32)
    upper = at_row <= at_col
    m[:, :BLOCK] = gt[:, :BLOCK]
    m[:, BLOCK:] = eye
    eliminate(m)
    w0 = m[:, BLOCK:]
    r00 = jnp.where(upper, m[:, :BLOCK], 0.0)
    r01 = mm(w0, gt[:, BLOCK:WIDE])
    r0j = mm(w0, gt[:, WIDE:])
    m[:, :BLOCK] = gb[:, :BLOCK] - mm(r01, r01, 0, 0)
    m[:, BLOCK:] = eye
    eliminate(m)
    w1 = m[:, BLOCK:]
    r11 = jnp.where(upper, m[:, :BLOCK], 0.0)
    r1j = mm(w1, gb[:, BLOCK:] - mm(r01, r0j, 0, 0))
    zero, one = c == 0, c == 1
    rr[:BLOCK, :] = jnp.where(zero, r00, jnp.where(one, r01, r0j))
    rr[BLOCK:, :] = jnp.where(zero, 0.0, jnp.where(one, r11, r1j))

    def tail(k, carry):
        at = pl.ds(pl.multiple_of(k * chunk, chunk), chunk)
        q0 = mm(pan[at, :BLOCK], w0, 1, 1)
        q1 = mm(pan[at, BLOCK:] - mm(q0, r01), w1, 1, 1)
        later = own[at, :] - mm(q0, r0j) - mm(q1, r1j)
        fac[at, :] = jnp.where(zero, q0 * stretch, jnp.where(one, q1 * stretch, later))
        return carry

    lax.fori_loop(0, pan.shape[0] // chunk, tail, 0)


def shards(n_col, n_row, jacobian, counts):
    rows_dev, width = jacobian.shape
    assert width == n_col * BLOCK and n_row == 4
    local = n_col * rows_dev
    chunk = min(256, local)
    stretch = math.sqrt(local * n_row)
    vmem = pl.BlockSpec(memory_space=pltpu.VMEM)
    shape = lambda *dims: jax.ShapeDtypeStruct(dims, F32)
    limit = 48 * 1024 * 1024
    pan, own, gt, gb = pl.pallas_call(
        functools.partial(exchange_kernel, n_col, chunk),
        out_shape=(
            shape(local, WIDE), shape(local, BLOCK), shape(BLOCK, 3 * BLOCK), shape(BLOCK, WIDE),
        ),
        in_specs=[vmem] * 2,
        out_specs=(vmem,) * 4,
        scratch_shapes=[
            pltpu.VMEM((rows_dev, width), F32),
            pltpu.VMEM((BLOCK, 3 * BLOCK), F32),
            pltpu.VMEM((BLOCK, WIDE), F32),
            pltpu.VMEM((HALF, 3 * BLOCK), F32),
            pltpu.VMEM((HALF, WIDE), F32),
            pltpu.VMEM((HALF, 3 * BLOCK), F32),
            pltpu.VMEM((HALF, WIDE), F32),
            pltpu.VMEM((HALF, 3 * BLOCK), F32),
            pltpu.VMEM((HALF, WIDE), F32),
            pltpu.SemaphoreType.DMA((n_col,)),
            pltpu.SemaphoreType.DMA((n_col,)),
            pltpu.SemaphoreType.DMA((n_col,)),
            pltpu.SemaphoreType.DMA((n_col,)),
            pltpu.SemaphoreType.DMA((6,)),
            pltpu.SemaphoreType.DMA((6,)),
        ],
        compiler_params=pltpu.CompilerParams(
            collective_id=0, has_side_effects=True, vmem_limit_bytes=limit
        ),
    )(jacobian, counts.reshape(1, rows_dev))
    fac, rr = pl.pallas_call(
        functools.partial(finish_kernel, n_col, stretch, chunk),
        out_shape=(shape(local, BLOCK), shape(WIDE, BLOCK)),
        in_specs=[vmem] * 4,
        out_specs=(vmem,) * 2,
        scratch_shapes=[pltpu.VMEM((BLOCK, WIDE), F32)],
        compiler_params=pltpu.CompilerParams(vmem_limit_bytes=limit),
    )(pan, own, gt, gb)
    factored = fac.reshape(n_col, 1, rows_dev, 1, 1, BLOCK)
    return (factored, rr.reshape(WIDE, 1, 1, BLOCK))


def solution(mesh):
    placed = (P(("col", "row"), None), P(("col", "row")))
    return jax.shard_map(
        functools.partial(shards, mesh.shape["col"], mesh.shape["row"]),
        mesh=mesh,
        in_specs=placed,
        out_specs=(P(None, "row", None, None, "col", None), P(None, None, "col", None)),
        check_vma=False,
    )
```

```python
import functools
import math

import jax
import jax.numpy as jnp
from jax import lax
from jax.experimental import pallas as pl
from jax.experimental.pallas import tpu as pltpu
from jax.sharding import PartitionSpec as P

BLOCK = 128
WIDE = 2 * BLOCK
HALF = BLOCK // 2
STEP = 16
B16 = jnp.bfloat16
HIGH = lax.Precision.HIGHEST
MESH = pl.DeviceIdType.MESH
F32 = jnp.float32


def mm(a, b, ca=1, cb=0):
    return lax.dot_general(
        a, b, (((ca,), (cb,)), ((), ())), precision=HIGH, preferred_element_type=F32
    )


def split3(x):
    high = x.astype(B16)
    x = x - high.astype(F32)
    mid = x.astype(B16)
    return high, mid, (x - mid.astype(F32)).astype(B16)


def outer(rows):
    h, m, l = split3(rows)
    lh, lm, ll = h[:, :BLOCK], m[:, :BLOCK], l[:, :BLOCK]
    a = jnp.concatenate([lh, lh, lm, lh, ll, lm], axis=0)
    b = jnp.concatenate([h, m, h, l, h, m], axis=0)
    return lax.dot_general(a, b, (((0,), (0,)), ((), ())), preferred_element_type=F32)


def recip(x):
    guess = pl.reciprocal(x, approx=True)
    return guess * (2.0 - x * guess)


def eliminate(m, hooks):
    row = lax.broadcasted_iota(jnp.int32, (STEP, BLOCK), 0)
    for kb in range(BLOCK // STEP):
        r0 = STEP * kb
        left = m[r0 : r0 + STEP, :BLOCK]
        right = m[r0 : r0 + STEP, BLOCK:]
        cols = [
            jnp.broadcast_to(left[:, r0 + k : r0 + k + 1], (STEP, BLOCK)) for k in range(STEP)
        ]
        diag = jnp.zeros((STEP, BLOCK), F32)
        for k in range(0, STEP, 2):
            c1, c2 = cols[k], cols[k + 1]
            a, b, e = c1[k : k + 1, :], c1[k + 1 : k + 2, :], c2[k + 1 : k + 2, :]
            g = b * recip(a)
            diag = jnp.where(row == k, a, jnp.where(row == k + 1, e - b * g, diag))
            l1, l2 = left[k : k + 1, :], left[k + 1 : k + 2, :]
            q1, q2 = right[k : k + 1, :], right[k + 1 : k + 2, :]
            f1 = jnp.where(row == k + 1, g, 0.0)
            if k < STEP - 2:
                inv = recip(a * e - b * b)
                below = row > k + 1
                f2 = jnp.where(below, (a * c2 - b * c1) * inv, 0.0)
                f1 = jnp.where(below, (e * c1 - b * c2) * inv, f1)
                for j in range(k + 2, STEP):
                    cols[j] = cols[j] - f1 * cols[j][k : k + 1, :] - f2 * cols[j][k + 1 : k + 2, :]
                left = left - f2 * l2
                right = right - f2 * q2
            left = left - f1 * l1
            right = right - f1 * q1
        scale = lax.rsqrt(diag)
        left = left * scale
        right = right * scale
        m[r0 : r0 + STEP, :BLOCK] = left
        m[r0 : r0 + STEP, BLOCK:] = right
        if kb < BLOCK // STEP - 1:
            after = outer(jnp.concatenate([left, right], axis=1))
            m[r0 + STEP :, :] -= after[r0 + STEP :, :]
        if kb in hooks:
            hooks[kb]()


def kernel(
    n_col, stretch, chunk, jac_any, cnt_any, fac, rr,
    jac, cnt, sc, pan0, pan1, own, g0, in0, out0,
    part1, in1, half1, out1, g1, part2, in2, half2, out2, g2, m, r0j, u1j,
    load, send_p0, recv_p0, send_p1, recv_p1, send_a, recv_a, send_r, recv_r,
):
    rows = jac.shape[0]
    local = pan0.shape[0]
    c = lax.axis_index("col")
    r = lax.axis_index("row")
    core = lax.rem(r, 2)
    sib = r + 1 - 2 * core
    across = lax.rem(r + 2, 4)
    slant = sib + 2 - 4 * (sib // 2)

    loads = [
        pltpu.make_async_copy(jac_any, jac, load.at[0]),
        pltpu.make_async_copy(cnt_any, cnt, load.at[1]),
    ]
    for copy in loads:
        copy.start()
    barrier = pltpu.get_barrier_semaphore()

    def loop(body):
        def step(i, carry):
            body(i)
            return carry

        lax.fori_loop(1, n_col, step, 0)

    loop(
        lambda i: pl.semaphore_signal(
            barrier, inc=1, device_id=(lax.rem(c + i, n_col), r), device_id_type=MESH
        )
    )
    for other in (sib, across, slant):
        pl.semaphore_signal(barrier, inc=1, device_id=(c, other), device_id_type=MESH)
    for copy in loads:
        copy.wait()

    root = jnp.sqrt(cnt[...].astype(F32))
    spread = jnp.broadcast_to(root, (rows, rows))
    eye_rows = lax.broadcasted_iota(jnp.int32, (rows, rows), 0) == lax.broadcasted_iota(
        jnp.int32, (rows, rows), 1
    )
    column = jnp.sum(jnp.where(eye_rows, spread, 0.0), axis=1, keepdims=True)
    sc[...] = jac[...] * column
    mine = pl.ds(pl.multiple_of(c * rows, rows), rows)

    pl.semaphore_wait(barrier, n_col + 2)

    def sender(dst, send, recv, lanes_of):
        def make(i):
            t = lax.rem(c + i, n_col)
            return pltpu.make_async_remote_copy(
                src_ref=sc.at[:, lanes_of(t)],
                dst_ref=dst.at[mine, :],
                send_sem=send.at[i],
                recv_sem=recv.at[i],
                device_id=(t, r),
                device_id_type=MESH,
            )

        return make

    block_of = lambda t: pl.ds(pl.multiple_of(t * BLOCK, BLOCK), BLOCK)
    send_first = sender(pan0, send_p0, recv_p0, lambda t: pl.ds(0, BLOCK))
    send_second = sender(pan1, send_p1, recv_p1, lambda t: pl.ds(BLOCK, BLOCK))
    send_own = sender(own, send_a, recv_a, block_of)
    loop(lambda i: send_first(i).start())
    loop(lambda i: send_second(i).start())
    loop(lambda i: send_own(i).start())
    pan0[mine, :] = sc[:, :BLOCK]
    pan1[mine, :] = sc[:, BLOCK:WIDE]
    own[mine, :] = sc[:, block_of(c)]

    def gram(out, lanes, x, y):
        if local == chunk:
            out[:, lanes] = mm(x[...], y[...], 0, 0)
            return
        out[:, lanes] = jnp.zeros((BLOCK, BLOCK), F32)

        def add(k, carry):
            at = pl.ds(pl.multiple_of(k * chunk, chunk), chunk)
            out[:, lanes] += mm(x[at, :], y[at, :], 0, 0)
            return carry

        lax.fori_loop(0, local // chunk, add, 0)

    def tiles(body):
        def step(k, carry):
            body(pl.ds(pl.multiple_of(k * chunk, chunk), chunk))
            return carry

        if local == chunk:
            body(pl.ds(0, chunk))
        else:
            lax.fori_loop(0, local // chunk, step, 0)

    first, second = slice(0, BLOCK), slice(BLOCK, WIDE)
    here = pl.ds(pl.multiple_of(core * HALF, HALF), HALF)
    there = pl.ds(pl.multiple_of((1 - core) * HALF, HALF), HALF)
    started = []

    def swap(src, dst, slot, other):
        copy = pltpu.make_async_remote_copy(
            src_ref=src,
            dst_ref=dst,
            send_sem=send_r.at[slot],
            recv_sem=recv_r.at[slot],
            device_id=(c, other),
            device_id_type=MESH,
        )
        copy.start()
        started.append(copy)
        return copy

    loop(lambda i: send_first(i).wait_recv())
    gram(g0, first, pan0, pan0)
    pair = swap(g0, in0, 0, sib)
    pair.wait()
    started.remove(pair)
    g0[...] += in0[...]
    straight = swap(g0.at[here, :], out0.at[here, :], 1, across)
    slanted = swap(g0.at[here, :], out0.at[here, :], 2, slant)

    box = {}

    def reduce_a(key, part, into, slot):
        box[key] = swap(part.at[there, :], into, slot, sib)

    def reduce_b(key, part, into, half, out, slot):
        box[key].wait_recv()
        half[...] = part[here, :] + into[...]
        box[key] = swap(half, out, slot, across)

    def reduce_c(key, half, out, total, slot):
        box[key].wait_recv()
        total[here, :] = half[...] + out[...]
        box[key] = swap(total.at[here, :], total.at[here, :], slot, sib)

    loop(lambda i: send_second(i).wait_recv())
    gram(part1, first, pan0, pan1)
    gram(part1, second, pan1, pan1)
    reduce_a(1, part1, in1, 3)
    straight.wait_recv()
    slanted.wait_recv()

    at_row = lax.broadcasted_iota(jnp.int32, (BLOCK, BLOCK), 0)
    at_col = lax.broadcasted_iota(jnp.int32, (BLOCK, BLOCK), 1)
    eye = jnp.where(at_row == at_col, 1.0, 0.0).astype(F32)
    upper = at_row <= at_col
    m[:, :BLOCK] = g0[...] + out0[...]
    m[:, BLOCK:] = eye

    def own_gram():
        loop(lambda i: send_own(i).wait_recv())
        gram(part2, first, pan0, own)
        gram(part2, second, pan1, own)
        reduce_a(2, part2, in2, 4)

    eliminate(
        m,
        {
            0: lambda: reduce_b(1, part1, in1, half1, out1, 5),
            2: own_gram,
            4: lambda: reduce_c(1, half1, out1, g1, 6),
            5: lambda: reduce_b(2, part2, in2, half2, out2, 7),
        },
    )
    w0 = m[:, BLOCK:]
    r00 = jnp.where(upper, m[:, :BLOCK], 0.0)
    box[1].wait_recv()
    r01 = mm(w0, g1[:, :BLOCK])
    m[:, :BLOCK] = g1[:, BLOCK:] - mm(r01, r01, 0, 0)
    m[:, BLOCK:] = eye
    zero, one = c == 0, c == 1

    def basis():
        def tile(at):
            q0 = mm(pan0[at, :], w0, 1, 1)
            pan0[at, :] = q0
            pan1[at, :] = pan1[at, :] - mm(q0, r01)

        tiles(tile)

    def coupling():
        box[2].wait_recv()
        r0j[...] = mm(w0, g2[:, :BLOCK])
        u1j[...] = g2[:, BLOCK:] - mm(r01, r0j[...], 0, 0)
        rr[:BLOCK, :] = jnp.where(zero, r00, jnp.where(one, r01, r0j[...]))

    def update():
        def tile(at):
            own[at, :] = own[at, :] - mm(pan0[at, :], r0j[...])

        tiles(tile)

    eliminate(
        m,
        {
            0: lambda: reduce_c(2, half2, out2, g2, 8),
            1: basis,
            3: coupling,
            4: update,
        },
    )
    w1 = m[:, BLOCK:]
    r11 = jnp.where(upper, m[:, :BLOCK], 0.0)
    r1j = mm(w1, u1j[...])
    rr[BLOCK:, :] = jnp.where(zero, 0.0, jnp.where(one, r11, r1j))

    def tail(at):
        q1 = mm(pan1[at, :], w1, 1, 1)
        later = own[at, :] - mm(q1, r1j)
        fac[at, :] = jnp.where(
            zero, pan0[at, :] * stretch, jnp.where(one, q1 * stretch, later)
        )

    tiles(tail)
    for copy in started:
        copy.wait_send()
    loop(lambda i: send_first(i).wait_send())
    loop(lambda i: send_second(i).wait_send())
    loop(lambda i: send_own(i).wait_send())


def shards(n_col, n_row, jacobian, counts):
    rows_dev, width = jacobian.shape
    assert width == n_col * BLOCK and n_row == 4
    local = n_col * rows_dev
    chunk = min(256, local)
    stretch = math.sqrt(local * n_row)
    vmem = pl.BlockSpec(memory_space=pltpu.VMEM)
    anywhere = pl.BlockSpec(memory_space=pl.ANY)
    shape = lambda *dims: jax.ShapeDtypeStruct(dims, F32)
    buf = lambda *dims: pltpu.VMEM(dims, F32)
    sems = pltpu.SemaphoreType.DMA((n_col,))
    staged = [
        buf(BLOCK, WIDE), buf(HALF, WIDE), buf(HALF, WIDE), buf(HALF, WIDE), buf(BLOCK, WIDE),
    ]
    fac, rr = pl.pallas_call(
        functools.partial(kernel, n_col, stretch, chunk),
        out_shape=(shape(local, BLOCK), shape(WIDE, BLOCK)),
        in_specs=[anywhere] * 2,
        out_specs=(vmem,) * 2,
        scratch_shapes=[
            buf(rows_dev, width), pltpu.VMEM((1, rows_dev), jnp.int32), buf(rows_dev, width),
            buf(local, BLOCK), buf(local, BLOCK), buf(local, BLOCK),
            buf(BLOCK, BLOCK), buf(BLOCK, BLOCK), buf(BLOCK, BLOCK),
            *staged, *staged, buf(BLOCK, WIDE), buf(BLOCK, BLOCK), buf(BLOCK, BLOCK),
            pltpu.SemaphoreType.DMA((2,)), sems, sems, sems, sems, sems, sems,
            pltpu.SemaphoreType.DMA((9,)), pltpu.SemaphoreType.DMA((9,)),
        ],
        compiler_params=pltpu.CompilerParams(
            collective_id=0, has_side_effects=True, vmem_limit_bytes=56 * 1024 * 1024
        ),
    )(jacobian, counts.reshape(1, rows_dev))
    factored = fac.reshape(n_col, 1, rows_dev, 1, 1, BLOCK)
    return (factored, rr.reshape(WIDE, 1, 1, BLOCK))


def solution(mesh):
    placed = (P(("col", "row"), None), P(("col", "row")))
    return jax.shard_map(
        functools.partial(shards, mesh.shape["col"], mesh.shape["row"]),
        mesh=mesh,
        in_specs=placed,
        out_specs=(P(None, "row", None, None, "col", None), P(None, None, "col", None)),
        check_vma=False,
    )
```

```python
import functools
import math

import jax
import jax.numpy as jnp
from jax import lax
from jax.experimental import pallas as pl
from jax.experimental.pallas import tpu as pltpu
from jax.sharding import PartitionSpec as P

BLOCK = 128
WIDE = 2 * BLOCK
HALF = BLOCK // 2
PACK = HALF + HALF // 2
STEP = 16
B16 = jnp.bfloat16
HIGH = lax.Precision.HIGHEST
MESH = pl.DeviceIdType.MESH
F32 = jnp.float32


def mm(a, b, ca=1, cb=0):
    return lax.dot_general(
        a, b, (((ca,), (cb,)), ((), ())), precision=HIGH, preferred_element_type=F32
    )


def split3(x):
    high = x.astype(B16)
    x = x - high.astype(F32)
    mid = x.astype(B16)
    return high, mid, (x - mid.astype(F32)).astype(B16)


def outer(rows):
    h, m, l = split3(rows)
    lh, lm, ll = h[:, :BLOCK], m[:, :BLOCK], l[:, :BLOCK]
    a = jnp.concatenate([lh, lh, lm, lh, ll, lm], axis=0)
    b = jnp.concatenate([h, m, h, l, h, m], axis=0)
    return lax.dot_general(a, b, (((0,), (0,)), ((), ())), preferred_element_type=F32)


def recip(x):
    guess = pl.reciprocal(x, approx=True)
    return guess * (2.0 - x * guess)


def eliminate(m, hooks):
    row = lax.broadcasted_iota(jnp.int32, (STEP, BLOCK), 0)
    for kb in range(BLOCK // STEP):
        r0 = STEP * kb
        left = m[r0 : r0 + STEP, :BLOCK]
        right = m[r0 : r0 + STEP, BLOCK:]
        cols = [
            jnp.broadcast_to(left[:, r0 + k : r0 + k + 1], (STEP, BLOCK)) for k in range(STEP)
        ]
        diag = jnp.zeros((STEP, BLOCK), F32)
        for k in range(0, STEP, 2):
            c1, c2 = cols[k], cols[k + 1]
            a, b, e = c1[k : k + 1, :], c1[k + 1 : k + 2, :], c2[k + 1 : k + 2, :]
            g = b * recip(a)
            diag = jnp.where(row == k, a, jnp.where(row == k + 1, e - b * g, diag))
            l1, l2 = left[k : k + 1, :], left[k + 1 : k + 2, :]
            q1, q2 = right[k : k + 1, :], right[k + 1 : k + 2, :]
            f1 = jnp.where(row == k + 1, g, 0.0)
            if k < STEP - 2:
                inv = recip(a * e - b * b)
                below = row > k + 1
                f2 = jnp.where(below, (a * c2 - b * c1) * inv, 0.0)
                f1 = jnp.where(below, (e * c1 - b * c2) * inv, f1)
                for j in range(k + 2, STEP):
                    cols[j] = cols[j] - f1 * cols[j][k : k + 1, :] - f2 * cols[j][k + 1 : k + 2, :]
                left = left - f2 * l2
                right = right - f2 * q2
            left = left - f1 * l1
            right = right - f1 * q1
        scale = lax.rsqrt(diag)
        left = left * scale
        right = right * scale
        m[r0 : r0 + STEP, :BLOCK] = left
        m[r0 : r0 + STEP, BLOCK:] = right
        if kb < BLOCK // STEP - 1:
            after = outer(jnp.concatenate([left, right], axis=1))
            m[r0 + STEP :, :] -= after[r0 + STEP :, :]
        if kb in hooks:
            hooks[kb]()


def kernel(
    n_col, stretch, chunk, jac_any, cnt_any, x1_out, x2_out, top_out, m_out, u_out,
    jac, cnt, sc, pan0, pan1, own, g0, pack, in0, out0, top,
    part1, in1, half1, out1, g1, part2, in2, half2, out2, g2, m, r0j, u1j,
    load, store, send_p0, recv_p0, send_p1, recv_p1, send_a, recv_a, send_r, recv_r,
):
    rows = jac.shape[0]
    local = pan0.shape[0]
    c = lax.axis_index("col")
    r = lax.axis_index("row")
    core = lax.rem(r, 2)
    sib = r + 1 - 2 * core
    across = lax.rem(r + 2, 4)
    slant = sib + 2 - 4 * (sib // 2)

    loads = [
        pltpu.make_async_copy(jac_any, jac, load.at[0]),
        pltpu.make_async_copy(cnt_any, cnt, load.at[1]),
    ]
    for copy in loads:
        copy.start()
    barrier = pltpu.get_barrier_semaphore()

    def loop(body):
        def step(i, carry):
            body(i)
            return carry

        lax.fori_loop(1, n_col, step, 0)

    loop(
        lambda i: pl.semaphore_signal(
            barrier, inc=1, device_id=(lax.rem(c + i, n_col), r), device_id_type=MESH
        )
    )
    for other in (sib, across, slant):
        pl.semaphore_signal(barrier, inc=1, device_id=(c, other), device_id_type=MESH)
    for copy in loads:
        copy.wait()

    root = jnp.sqrt(cnt[...].astype(F32))
    spread = jnp.broadcast_to(root, (rows, rows))
    eye_rows = lax.broadcasted_iota(jnp.int32, (rows, rows), 0) == lax.broadcasted_iota(
        jnp.int32, (rows, rows), 1
    )
    column = jnp.sum(jnp.where(eye_rows, spread, 0.0), axis=1, keepdims=True)
    sc[...] = jac[...] * column
    mine = pl.ds(pl.multiple_of(c * rows, rows), rows)

    pl.semaphore_wait(barrier, n_col + 2)

    def sender(dst, send, recv, lanes_of):
        def make(i):
            t = lax.rem(c + i, n_col)
            return pltpu.make_async_remote_copy(
                src_ref=sc.at[:, lanes_of(t)],
                dst_ref=dst.at[mine, :],
                send_sem=send.at[i],
                recv_sem=recv.at[i],
                device_id=(t, r),
                device_id_type=MESH,
            )

        return make

    block_of = lambda t: pl.ds(pl.multiple_of(t * BLOCK, BLOCK), BLOCK)
    send_first = sender(pan0, send_p0, recv_p0, lambda t: pl.ds(0, BLOCK))
    send_second = sender(pan1, send_p1, recv_p1, lambda t: pl.ds(BLOCK, BLOCK))
    send_own = sender(own, send_a, recv_a, block_of)
    loop(lambda i: send_first(i).start())
    pan0[mine, :] = sc[:, :BLOCK]
    pan1[mine, :] = sc[:, BLOCK:WIDE]
    own[mine, :] = sc[:, block_of(c)]

    def gram(out, lanes, x, y):
        if local == chunk:
            out[:, lanes] = mm(x[...], y[...], 0, 0)
            return
        out[:, lanes] = jnp.zeros((BLOCK, BLOCK), F32)

        def add(k, carry):
            at = pl.ds(pl.multiple_of(k * chunk, chunk), chunk)
            out[:, lanes] += mm(x[at, :], y[at, :], 0, 0)
            return carry

        lax.fori_loop(0, local // chunk, add, 0)

    def tiles(body):
        def step(k, carry):
            body(pl.ds(pl.multiple_of(k * chunk, chunk), chunk))
            return carry

        if local == chunk:
            body(pl.ds(0, chunk))
        else:
            lax.fori_loop(0, local // chunk, step, 0)

    first, second = slice(0, BLOCK), slice(BLOCK, WIDE)
    here = pl.ds(pl.multiple_of(core * HALF, HALF), HALF)
    there = pl.ds(pl.multiple_of((1 - core) * HALF, HALF), HALF)
    started = []

    def swap(src, dst, slot, other):
        copy = pltpu.make_async_remote_copy(
            src_ref=src,
            dst_ref=dst,
            send_sem=send_r.at[slot],
            recv_sem=recv_r.at[slot],
            device_id=(c, other),
            device_id_type=MESH,
        )
        copy.start()
        started.append(copy)
        return copy

    loop(lambda i: send_first(i).wait_recv())
    loop(lambda i: send_second(i).start())
    gram(g0, first, pan0, pan0)
    low_lane = lax.broadcasted_iota(jnp.int32, (PACK - HALF, BLOCK), 1) < HALF
    pack[:HALF, :] = g0[:HALF, :]
    pack[HALF:, :] = jnp.where(low_lane, pltpu.roll(g0[PACK:, :], HALF, 1), g0[HALF:PACK, :])
    pair = swap(pack, in0, 0, sib)
    pair.wait()
    started.remove(pair)
    pack[...] += in0[...]
    part = pl.ds(pl.multiple_of(core * (PACK // 2), PACK // 2), PACK // 2)
    straight = swap(pack.at[part, :], out0.at[part, :], 1, across)
    slanted = swap(pack.at[part, :], out0.at[part, :], 2, slant)

    box = {}

    def reduce_a(key, part, into, slot):
        box[key] = swap(part.at[there, :], into, slot, sib)

    def reduce_b(key, part, into, half, out, slot):
        box[key].wait_recv()
        half[...] = part[here, :] + into[...]
        box[key] = swap(half, out, slot, across)

    def reduce_c(key, half, out, total, slot):
        box[key].wait_recv()
        total[here, :] = half[...] + out[...]
        box[key] = swap(total.at[here, :], total.at[here, :], slot, sib)

    loop(lambda i: send_second(i).wait_recv())
    gram(part1, first, pan0, pan1)
    gram(part1, second, pan1, pan1)
    loop(lambda i: send_own(i).start())
    reduce_a(1, part1, in1, 3)
    straight.wait_recv()
    slanted.wait_recv()

    at_row = lax.broadcasted_iota(jnp.int32, (BLOCK, BLOCK), 0)
    at_col = lax.broadcasted_iota(jnp.int32, (BLOCK, BLOCK), 1)
    eye = jnp.where(at_row == at_col, 1.0, 0.0).astype(F32)
    upper = at_row <= at_col
    low = pack[HALF:, :] + out0[HALF:, :]
    m[:HALF, :BLOCK] = pack[:HALF, :] + out0[:HALF, :]
    m[HALF:PACK, :BLOCK] = low
    m[PACK:, :BLOCK] = pltpu.roll(low, HALF, 1)
    m[:, BLOCK:] = eye

    def own_gram():
        loop(lambda i: send_own(i).wait_recv())
        gram(part2, first, pan0, own)
        gram(part2, second, pan1, own)
        reduce_a(2, part2, in2, 4)

    eliminate(
        m,
        {
            0: lambda: reduce_b(1, part1, in1, half1, out1, 5),
            4: lambda: reduce_c(1, half1, out1, g1, 6),
            5: own_gram,
        },
    )
    w0 = m[:, BLOCK:]
    r00 = jnp.where(upper, m[:, :BLOCK], 0.0)
    box[1].wait_recv()
    r01 = mm(w0, g1[:, :BLOCK])
    m[:, :BLOCK] = g1[:, BLOCK:] - mm(r01, r01, 0, 0)
    m[:, BLOCK:] = eye
    zero, one = c == 0, c == 1

    saved = []

    def save(src, dst, slot):
        copy = pltpu.make_async_copy(src, dst, store.at[slot])
        copy.start()
        saved.append(copy)

    def basis():
        def tile(at):
            q0 = mm(pan0[at, :], w0, 1, 1)
            pan0[at, :] = q0
            pan1[at, :] = pan1[at, :] - mm(q0, r01)

        tiles(tile)
        save(pan1, x1_out, 0)

    def coupling():
        box[2].wait_recv()
        r0j[...] = mm(w0, g2[:, :BLOCK])
        u1j[...] = g2[:, BLOCK:] - mm(r01, r0j[...], 0, 0)
        top[...] = jnp.where(zero, r00, jnp.where(one, r01, r0j[...]))
        save(top, top_out, 1)
        save(u1j, u_out, 2)

    def update():
        def tile(at):
            q0 = pan0[at, :]
            own[at, :] = jnp.where(zero, q0 * stretch, own[at, :] - mm(q0, r0j[...]))

        tiles(tile)
        save(own, x2_out, 3)

    eliminate(
        m,
        {
            0: lambda: reduce_b(2, part2, in2, half2, out2, 7),
            1: basis,
            3: lambda: reduce_c(2, half2, out2, g2, 8),
            5: coupling,
            6: update,
        },
    )
    save(m, m_out, 4)
    for copy in saved:
        copy.wait()
    for copy in started:
        copy.wait_send()
    loop(lambda i: send_first(i).wait_send())
    loop(lambda i: send_second(i).wait_send())
    loop(lambda i: send_own(i).wait_send())


def finish(
    stretch, chunk, x1_any, x2_any, top_any, m_any, u_any, fac, rr, x1, x2, m, u1j, load
):
    pairs = [(m_any, m), (u_any, u1j), (x1_any, x1), (x2_any, x2), (top_any, rr.at[:BLOCK, :])]
    loads = [pltpu.make_async_copy(a, b, load.at[k]) for k, (a, b) in enumerate(pairs)]
    for copy in loads:
        copy.start()
    c = lax.axis_index("col")
    zero, one = c == 0, c == 1
    loads[0].wait()
    loads[1].wait()
    w1 = m[:, BLOCK:]
    upper = lax.broadcasted_iota(jnp.int32, (BLOCK, BLOCK), 0) <= lax.broadcasted_iota(
        jnp.int32, (BLOCK, BLOCK), 1
    )
    r1j = mm(w1, u1j[...])
    r11 = jnp.where(upper, m[:, :BLOCK], 0.0)
    rr[BLOCK:, :] = jnp.where(zero, 0.0, jnp.where(one, r11, r1j))

    loads[2].wait()
    loads[3].wait()

    def tail(k, carry):
        at = pl.ds(pl.multiple_of(k * chunk, chunk), chunk)
        q1 = mm(x1[at, :], w1, 1, 1)
        later = x2[at, :] - mm(q1, r1j)
        fac[at, :] = jnp.where(zero, x2[at, :], jnp.where(one, q1 * stretch, later))
        return carry

    lax.fori_loop(0, x1.shape[0] // chunk, tail, 0)
    loads[4].wait()


def shards(n_col, n_row, jacobian, counts):
    rows_dev, width = jacobian.shape
    assert width == n_col * BLOCK and n_row == 4
    local = n_col * rows_dev
    chunk = min(256, local)
    stretch = math.sqrt(local * n_row)
    vmem = pl.BlockSpec(memory_space=pltpu.VMEM)
    anywhere = pl.BlockSpec(memory_space=pl.ANY)
    shape = lambda *dims: jax.ShapeDtypeStruct(dims, F32)
    buf = lambda *dims: pltpu.VMEM(dims, F32)
    sems = pltpu.SemaphoreType.DMA((n_col,))
    staged = [
        buf(BLOCK, WIDE), buf(HALF, WIDE), buf(HALF, WIDE), buf(HALF, WIDE), buf(BLOCK, WIDE),
    ]
    states = pl.pallas_call(
        functools.partial(kernel, n_col, stretch, chunk),
        out_shape=(
            shape(local, BLOCK), shape(local, BLOCK), shape(BLOCK, BLOCK), shape(BLOCK, WIDE),
            shape(BLOCK, BLOCK),
        ),
        in_specs=[anywhere] * 2,
        out_specs=(anywhere,) * 5,
        scratch_shapes=[
            buf(rows_dev, width), pltpu.VMEM((1, rows_dev), jnp.int32), buf(rows_dev, width),
            buf(local, BLOCK), buf(local, BLOCK), buf(local, BLOCK),
            buf(BLOCK, BLOCK), buf(PACK, BLOCK), buf(PACK, BLOCK), buf(PACK, BLOCK),
            buf(BLOCK, BLOCK), *staged, *staged, buf(BLOCK, WIDE), buf(BLOCK, BLOCK), buf(BLOCK, BLOCK),
            pltpu.SemaphoreType.DMA((2,)), pltpu.SemaphoreType.DMA((5,)), sems, sems, sems, sems, sems, sems,
            pltpu.SemaphoreType.DMA((9,)), pltpu.SemaphoreType.DMA((9,)),
        ],
        compiler_params=pltpu.CompilerParams(
            collective_id=0, has_side_effects=True, vmem_limit_bytes=56 * 1024 * 1024
        ),
    )(jacobian, counts.reshape(1, rows_dev))
    fac, rr = pl.pallas_call(
        functools.partial(finish, stretch, chunk),
        out_shape=(shape(local, BLOCK), shape(WIDE, BLOCK)),
        in_specs=[anywhere] * 5,
        out_specs=(vmem,) * 2,
        scratch_shapes=[
            buf(local, BLOCK), buf(local, BLOCK), buf(BLOCK, WIDE), buf(BLOCK, BLOCK),
            pltpu.SemaphoreType.DMA((5,)),
        ],
        compiler_params=pltpu.CompilerParams(vmem_limit_bytes=56 * 1024 * 1024),
    )(*states)
    factored = fac.reshape(n_col, 1, rows_dev, 1, 1, BLOCK)
    return (factored, rr.reshape(WIDE, 1, 1, BLOCK))


def solution(mesh):
    placed = (P(("col", "row"), None), P(("col", "row")))
    return jax.shard_map(
        functools.partial(shards, mesh.shape["col"], mesh.shape["row"]),
        mesh=mesh,
        in_specs=placed,
        out_specs=(P(None, "row", None, None, "col", None), P(None, None, "col", None)),
        check_vma=False,
    )
```

```python
import functools
import math

import jax
import jax.numpy as jnp
from jax import lax
from jax.experimental import pallas as pl
from jax.experimental.pallas import tpu as pltpu
from jax.sharding import PartitionSpec as P

BLOCK = 128
WIDE = 2 * BLOCK
HALF = BLOCK // 2
PACK = HALF + HALF // 2
STEP = 16
B16 = jnp.bfloat16
HIGH = lax.Precision.HIGHEST
MESH = pl.DeviceIdType.MESH
F32 = jnp.float32


def mm(a, b, ca=1, cb=0):
    return lax.dot_general(
        a, b, (((ca,), (cb,)), ((), ())), precision=HIGH, preferred_element_type=F32
    )


def split3(x):
    high = x.astype(B16)
    x = x - high.astype(F32)
    mid = x.astype(B16)
    return high, mid, (x - mid.astype(F32)).astype(B16)


def outer(rows):
    h, m, l = split3(rows)
    lh, lm, ll = h[:, :BLOCK], m[:, :BLOCK], l[:, :BLOCK]
    a = jnp.concatenate([lh, lh, lm, lh, ll, lm], axis=0)
    b = jnp.concatenate([h, m, h, l, h, m], axis=0)
    return lax.dot_general(a, b, (((0,), (0,)), ((), ())), preferred_element_type=F32)


def recip(x):
    guess = pl.reciprocal(x, approx=True)
    return guess * (2.0 - x * guess)


def eliminate(m, hooks):
    row = lax.broadcasted_iota(jnp.int32, (STEP, BLOCK), 0)
    for kb in range(BLOCK // STEP):
        r0 = STEP * kb
        left = m[r0 : r0 + STEP, :BLOCK]
        right = m[r0 : r0 + STEP, BLOCK:]
        cols = [
            jnp.broadcast_to(left[:, r0 + k : r0 + k + 1], (STEP, BLOCK)) for k in range(STEP)
        ]
        diag = jnp.zeros((STEP, BLOCK), F32)
        for k in range(0, STEP, 2):
            c1, c2 = cols[k], cols[k + 1]
            a, b, e = c1[k : k + 1, :], c1[k + 1 : k + 2, :], c2[k + 1 : k + 2, :]
            g = b * recip(a)
            diag = jnp.where(row == k, a, jnp.where(row == k + 1, e - b * g, diag))
            l1, l2 = left[k : k + 1, :], left[k + 1 : k + 2, :]
            q1, q2 = right[k : k + 1, :], right[k + 1 : k + 2, :]
            f1 = jnp.where(row == k + 1, g, 0.0)
            if k < STEP - 2:
                inv = recip(a * e - b * b)
                below = row > k + 1
                f2 = jnp.where(below, (a * c2 - b * c1) * inv, 0.0)
                f1 = jnp.where(below, (e * c1 - b * c2) * inv, f1)
                for j in range(k + 2, STEP):
                    cols[j] = cols[j] - f1 * cols[j][k : k + 1, :] - f2 * cols[j][k + 1 : k + 2, :]
                left = left - f2 * l2
                right = right - f2 * q2
            left = left - f1 * l1
            right = right - f1 * q1
        scale = lax.rsqrt(diag)
        left = left * scale
        right = right * scale
        m[r0 : r0 + STEP, :BLOCK] = left
        m[r0 : r0 + STEP, BLOCK:] = right
        if kb < BLOCK // STEP - 1:
            after = outer(jnp.concatenate([left, right], axis=1))
            m[r0 + STEP :, :] -= after[r0 + STEP :, :]
        if kb in hooks:
            hooks[kb]()


def kernel(
    n_col, stretch, chunk, jac_any, cnt_any, x1_out, x2_out, top_out, m_out, u_out,
    jac, cnt, sc, pan0, pan1, own, g0, pack, in0, out0, top,
    part1, in1, half1, out1, g1, part2, in2, half2, out2, g2, m, r0j, u1j,
    load, store, send_p0, recv_p0, send_p1, recv_p1, send_a, recv_a, send_r, recv_r,
):
    rows = jac.shape[0]
    local = pan0.shape[0]
    c = lax.axis_index("col")
    r = lax.axis_index("row")
    core = lax.rem(r, 2)
    sib = r + 1 - 2 * core
    across = lax.rem(r + 2, 4)
    slant = sib + 2 - 4 * (sib // 2)

    loads = [
        pltpu.make_async_copy(jac_any, jac, load.at[0]),
        pltpu.make_async_copy(cnt_any, cnt, load.at[1]),
    ]
    for copy in loads:
        copy.start()
    barrier = pltpu.get_barrier_semaphore()

    def loop(body):
        def step(i, carry):
            body(i)
            return carry

        lax.fori_loop(1, n_col, step, 0)

    loop(
        lambda i: pl.semaphore_signal(
            barrier, inc=1, device_id=(lax.rem(c + i, n_col), r), device_id_type=MESH
        )
    )
    for other in (sib, across, slant):
        pl.semaphore_signal(barrier, inc=1, device_id=(c, other), device_id_type=MESH)
    for copy in loads:
        copy.wait()

    root = jnp.sqrt(cnt[...].astype(F32))
    spread = jnp.broadcast_to(root, (rows, rows))
    eye_rows = lax.broadcasted_iota(jnp.int32, (rows, rows), 0) == lax.broadcasted_iota(
        jnp.int32, (rows, rows), 1
    )
    column = jnp.sum(jnp.where(eye_rows, spread, 0.0), axis=1, keepdims=True)
    sc[...] = jac[...] * column
    mine = pl.ds(pl.multiple_of(c * rows, rows), rows)

    pl.semaphore_wait(barrier, n_col + 2)

    def sender(dst, send, recv, lanes_of):
        def make(i):
            t = lax.rem(c + i, n_col)
            return pltpu.make_async_remote_copy(
                src_ref=sc.at[:, lanes_of(t)],
                dst_ref=dst.at[mine, :],
                send_sem=send.at[i],
                recv_sem=recv.at[i],
                device_id=(t, r),
                device_id_type=MESH,
            )

        return make

    block_of = lambda t: pl.ds(pl.multiple_of(t * BLOCK, BLOCK), BLOCK)
    send_first = sender(pan0, send_p0, recv_p0, lambda t: pl.ds(0, BLOCK))
    send_second = sender(pan1, send_p1, recv_p1, lambda t: pl.ds(BLOCK, BLOCK))
    send_own = sender(own, send_a, recv_a, block_of)
    loop(lambda i: send_first(i).start())
    loop(lambda i: send_second(i).start())
    pan0[mine, :] = sc[:, :BLOCK]
    pan1[mine, :] = sc[:, BLOCK:WIDE]
    own[mine, :] = sc[:, block_of(c)]

    def gram(out, lanes, x, y):
        if local == chunk:
            out[:, lanes] = mm(x[...], y[...], 0, 0)
            return
        out[:, lanes] = jnp.zeros((BLOCK, BLOCK), F32)

        def add(k, carry):
            at = pl.ds(pl.multiple_of(k * chunk, chunk), chunk)
            out[:, lanes] += mm(x[at, :], y[at, :], 0, 0)
            return carry

        lax.fori_loop(0, local // chunk, add, 0)

    def tiles(body):
        def step(k, carry):
            body(pl.ds(pl.multiple_of(k * chunk, chunk), chunk))
            return carry

        if local == chunk:
            body(pl.ds(0, chunk))
        else:
            lax.fori_loop(0, local // chunk, step, 0)

    first, second = slice(0, BLOCK), slice(BLOCK, WIDE)
    here = pl.ds(pl.multiple_of(core * HALF, HALF), HALF)
    there = pl.ds(pl.multiple_of((1 - core) * HALF, HALF), HALF)
    started = []

    def swap(src, dst, slot, other):
        copy = pltpu.make_async_remote_copy(
            src_ref=src,
            dst_ref=dst,
            send_sem=send_r.at[slot],
            recv_sem=recv_r.at[slot],
            device_id=(c, other),
            device_id_type=MESH,
        )
        copy.start()
        started.append(copy)
        return copy

    loop(lambda i: send_first(i).wait_recv())
    loop(lambda i: send_own(i).start())
    gram(g0, first, pan0, pan0)
    low_lane = lax.broadcasted_iota(jnp.int32, (PACK - HALF, BLOCK), 1) < HALF
    pack[:HALF, :] = g0[:HALF, :]
    pack[HALF:, :] = jnp.where(low_lane, pltpu.roll(g0[PACK:, :], HALF, 1), g0[HALF:PACK, :])
    pair = swap(pack, in0, 0, sib)
    pair.wait()
    started.remove(pair)
    pack[...] += in0[...]
    part = pl.ds(pl.multiple_of(core * (PACK // 2), PACK // 2), PACK // 2)
    straight = swap(pack.at[part, :], out0.at[part, :], 1, across)
    slanted = swap(pack.at[part, :], out0.at[part, :], 2, slant)

    box = {}

    def reduce_a(key, part, into, slot):
        box[key] = swap(part.at[there, :], into, slot, sib)

    def reduce_b(key, part, into, half, out, slot):
        box[key].wait_recv()
        half[...] = part[here, :] + into[...]
        box[key] = swap(half, out, slot, across)

    def reduce_c(key, half, out, total, slot):
        box[key].wait_recv()
        total[here, :] = half[...] + out[...]
        box[key] = swap(total.at[here, :], total.at[here, :], slot, sib)

    loop(lambda i: send_second(i).wait_recv())
    gram(part1, first, pan0, pan1)
    gram(part1, second, pan1, pan1)
    reduce_a(1, part1, in1, 3)
    straight.wait_recv()
    slanted.wait_recv()

    at_row = lax.broadcasted_iota(jnp.int32, (BLOCK, BLOCK), 0)
    at_col = lax.broadcasted_iota(jnp.int32, (BLOCK, BLOCK), 1)
    eye = jnp.where(at_row == at_col, 1.0, 0.0).astype(F32)
    upper = at_row <= at_col
    low = pack[HALF:, :] + out0[HALF:, :]
    m[:HALF, :BLOCK] = pack[:HALF, :] + out0[:HALF, :]
    m[HALF:PACK, :BLOCK] = low
    m[PACK:, :BLOCK] = pltpu.roll(low, HALF, 1)
    m[:, BLOCK:] = eye

    def own_gram():
        loop(lambda i: send_own(i).wait_recv())
        gram(part2, first, pan0, own)
        gram(part2, second, pan1, own)
        reduce_a(2, part2, in2, 4)

    eliminate(
        m,
        {
            0: lambda: reduce_b(1, part1, in1, half1, out1, 5),
            2: own_gram,
            4: lambda: reduce_c(1, half1, out1, g1, 6),
            5: lambda: reduce_b(2, part2, in2, half2, out2, 7),
        },
    )
    w0 = m[:, BLOCK:]
    r00 = jnp.where(upper, m[:, :BLOCK], 0.0)
    box[1].wait_recv()
    r01 = mm(w0, g1[:, :BLOCK])
    m[:, :BLOCK] = g1[:, BLOCK:] - mm(r01, r01, 0, 0)
    m[:, BLOCK:] = eye
    zero, one = c == 0, c == 1

    saved = []

    def save(src, dst, slot):
        copy = pltpu.make_async_copy(src, dst, store.at[slot])
        copy.start()
        saved.append(copy)

    def basis():
        def tile(at):
            q0 = mm(pan0[at, :], w0, 1, 1)
            pan0[at, :] = q0
            pan1[at, :] = pan1[at, :] - mm(q0, r01)

        tiles(tile)
        save(pan1, x1_out, 0)

    def coupling():
        box[2].wait_recv()
        r0j[...] = mm(w0, g2[:, :BLOCK])
        u1j[...] = g2[:, BLOCK:] - mm(r01, r0j[...], 0, 0)
        top[...] = jnp.where(zero, r00, jnp.where(one, r01, r0j[...]))
        save(top, top_out, 1)
        save(u1j, u_out, 2)

    def update():
        def tile(at):
            q0 = pan0[at, :]
            own[at, :] = jnp.where(zero, q0 * stretch, own[at, :] - mm(q0, r0j[...]))

        tiles(tile)
        save(own, x2_out, 3)

    eliminate(
        m,
        {
            0: lambda: reduce_c(2, half2, out2, g2, 8),
            1: basis,
            3: coupling,
            4: update,
        },
    )
    save(m, m_out, 4)
    for copy in saved:
        copy.wait()
    for copy in started:
        copy.wait_send()
    loop(lambda i: send_first(i).wait_send())
    loop(lambda i: send_second(i).wait_send())
    loop(lambda i: send_own(i).wait_send())


def finish(
    stretch, chunk, x1_any, x2_any, top_any, m_any, u_any, fac, rr, x1, x2, m, u1j, load
):
    pairs = [(m_any, m), (u_any, u1j), (x1_any, x1), (x2_any, x2), (top_any, rr.at[:BLOCK, :])]
    loads = [pltpu.make_async_copy(a, b, load.at[k]) for k, (a, b) in enumerate(pairs)]
    for copy in loads:
        copy.start()
    c = lax.axis_index("col")
    zero, one = c == 0, c == 1
    loads[0].wait()
    loads[1].wait()
    w1 = m[:, BLOCK:]
    upper = lax.broadcasted_iota(jnp.int32, (BLOCK, BLOCK), 0) <= lax.broadcasted_iota(
        jnp.int32, (BLOCK, BLOCK), 1
    )
    r1j = mm(w1, u1j[...])
    r11 = jnp.where(upper, m[:, :BLOCK], 0.0)
    rr[BLOCK:, :] = jnp.where(zero, 0.0, jnp.where(one, r11, r1j))

    loads[2].wait()
    loads[3].wait()

    def tail(k, carry):
        at = pl.ds(pl.multiple_of(k * chunk, chunk), chunk)
        q1 = mm(x1[at, :], w1, 1, 1)
        later = x2[at, :] - mm(q1, r1j)
        fac[at, :] = jnp.where(zero, x2[at, :], jnp.where(one, q1 * stretch, later))
        return carry

    lax.fori_loop(0, x1.shape[0] // chunk, tail, 0)
    loads[4].wait()


def shards(n_col, n_row, jacobian, counts):
    rows_dev, width = jacobian.shape
    assert width == n_col * BLOCK and n_row == 4
    local = n_col * rows_dev
    chunk = min(256, local)
    stretch = math.sqrt(local * n_row)
    vmem = pl.BlockSpec(memory_space=pltpu.VMEM)
    anywhere = pl.BlockSpec(memory_space=pl.ANY)
    shape = lambda *dims: jax.ShapeDtypeStruct(dims, F32)
    buf = lambda *dims: pltpu.VMEM(dims, F32)
    sems = pltpu.SemaphoreType.DMA((n_col,))
    staged = [
        buf(BLOCK, WIDE), buf(HALF, WIDE), buf(HALF, WIDE), buf(HALF, WIDE), buf(BLOCK, WIDE),
    ]
    states = pl.pallas_call(
        functools.partial(kernel, n_col, stretch, chunk),
        out_shape=(
            shape(local, BLOCK), shape(local, BLOCK), shape(BLOCK, BLOCK), shape(BLOCK, WIDE),
            shape(BLOCK, BLOCK),
        ),
        in_specs=[anywhere] * 2,
        out_specs=(anywhere,) * 5,
        scratch_shapes=[
            buf(rows_dev, width), pltpu.VMEM((1, rows_dev), jnp.int32), buf(rows_dev, width),
            buf(local, BLOCK), buf(local, BLOCK), buf(local, BLOCK),
            buf(BLOCK, BLOCK), buf(PACK, BLOCK), buf(PACK, BLOCK), buf(PACK, BLOCK),
            buf(BLOCK, BLOCK), *staged, *staged, buf(BLOCK, WIDE), buf(BLOCK, BLOCK), buf(BLOCK, BLOCK),
            pltpu.SemaphoreType.DMA((2,)), pltpu.SemaphoreType.DMA((5,)), sems, sems, sems, sems, sems, sems,
            pltpu.SemaphoreType.DMA((9,)), pltpu.SemaphoreType.DMA((9,)),
        ],
        compiler_params=pltpu.CompilerParams(
            collective_id=0, has_side_effects=True, vmem_limit_bytes=56 * 1024 * 1024
        ),
    )(jacobian, counts.reshape(1, rows_dev))
    fac, rr = pl.pallas_call(
        functools.partial(finish, stretch, chunk),
        out_shape=(shape(local, BLOCK), shape(WIDE, BLOCK)),
        in_specs=[anywhere] * 5,
        out_specs=(vmem,) * 2,
        scratch_shapes=[
            buf(local, BLOCK), buf(local, BLOCK), buf(BLOCK, WIDE), buf(BLOCK, BLOCK),
            pltpu.SemaphoreType.DMA((5,)),
        ],
        compiler_params=pltpu.CompilerParams(vmem_limit_bytes=56 * 1024 * 1024),
    )(*states)
    factored = fac.reshape(n_col, 1, rows_dev, 1, 1, BLOCK)
    return (factored, rr.reshape(WIDE, 1, 1, BLOCK))


def solution(mesh):
    placed = (P(("col", "row"), None), P(("col", "row")))
    return jax.shard_map(
        functools.partial(shards, mesh.shape["col"], mesh.shape["row"]),
        mesh=mesh,
        in_specs=placed,
        out_specs=(P(None, "row", None, None, "col", None), P(None, None, "col", None)),
        check_vma=False,
    )
```
